256 devices in a mesh: ex: 32 (over y_hi, z, core), lb: 8 (over y_lo, x).
Axes of the slice: x: 4, y: 4 (y_hi: 2, y_lo: 2; y = y_hi * 2 + y_lo), z: 8, core: 2. Of those that a mesh axis runs over, the one named last changes fastest.
Arguments:
- train_grads: bfloat16 [65536, 16384], P('ex', 'lb'), may hold values from -6 to 6
- query_grads: bfloat16 [1024, 16384], P('ex', 'lb'), may hold values from -0.046875 to 0.046875
- precond: bfloat16 [32, 512, 512], P('lb'), as said below
Outputs:
- scores: float32 [1024, 65536], P('lb', 'ex')
The draws below stay inside these ranges and needn't reach their ends.
Inputs may be any that keep to these rules, and one draw needn't show every extreme that they name: `precond`: each block is symmetric with its diagonal between 0.5 and 2.
All inputs are finite; a program needn't handle non-finite values.
Results may differ from the reference program's by a relative error of at most 0.015.
Values may be sent and summed in bfloat16 or wider, within the bound.
No kernel may reach another device: no remote copies, remote signals or barrier semaphores. Data moves between devices by JAX's collectives and lax.ppermute only.
A program may use at most 64 MiB of HBM per device.

```python
import jax
import jax.numpy as jnp
from jax import lax

BS = 512
BLOCKS_DEV = 4
BLOCKS = 32
WIDTH = 16384
NQ = 1024
NTRAIN = 65536
N_LB = 8


def draw_precond(key, part):
    key = jax.random.fold_in(key, 7)
    key_diag, key_off = jax.random.split(key)
    diag = jnp.exp(jax.random.uniform(key_diag, (BLOCKS, BS), jnp.float32, -0.69, 0.69))
    off = jax.random.normal(key_off, (BLOCKS, BS, BS), jnp.float32)
    off = off * (0.7 / BS ** 0.5)
    sym = 0.5 * (off + jnp.swapaxes(off, 1, 2))
    eye = jnp.eye(BS, dtype=jnp.float32)
    sym = sym * (1.0 - eye)[None, :, :] + eye[None, :, :] * diag[:, :, None]
    return sym.astype(jnp.bfloat16)


def levels(key, shape, cuts, low, top_value):
    def one(dim, blocks):
        heights = jax.random.uniform(jax.random.fold_in(jax.random.fold_in(key, 6), dim), (blocks,), jnp.float32, low / len(cuts), top_value / len(cuts))
        return jnp.repeat(jnp.exp(heights), shape[dim] // blocks).reshape((-1,) + (1,) * (len(shape) - dim - 1))

    loudness = one(*cuts[0])
    for cut in cuts[1:]:
        loudness = loudness * one(*cut)
    return loudness


def gaussian(own_key, extent, deviation, limit, shards=(), kind=jnp.bfloat16):
    result = deviation * jax.random.normal(own_key, extent, jnp.float32)
    if shards:
        result = result * levels(own_key, extent, shards, -0.22, 0.18)
    return jnp.clip(result, -limit, limit).astype(kind)


def setup_inputs(seed: int = 0) -> dict:
    key_of = jax.random.split(jax.random.key(seed), 4)
    return {
        "train_grads": gaussian(key_of[0], (NTRAIN, WIDTH), 1.0, 6.0, ((0, 32), (1, 8))),
        "query_grads": gaussian(key_of[1], (NQ, WIDTH), WIDTH ** -0.5, 0.046875, ((0, 32), (1, 8))),
        "precond": draw_precond(jax.random.fold_in(key_of[3], 71), 0),
    }


def prepare(rows, blocks):
    count = rows.shape[0]
    split = rows.reshape(count, blocks.shape[0], blocks.shape[1]).astype(jnp.float32)
    mixed = jnp.einsum("rbi,bij->rbj", split, blocks.astype(jnp.float32))
    return mixed.reshape(count, -1).astype(jnp.bfloat16)


def reference(train_grads, query_grads, precond):
    prepared = prepare(query_grads, precond)
    group_width = BLOCKS_DEV * BS
    query_groups = jnp.swapaxes(prepared.reshape(NQ, N_LB, group_width), 0, 1)
    train_groups = jnp.swapaxes(train_grads.reshape(NTRAIN, N_LB, group_width), 0, 1)

    def add_group(total, pieces):
        term = jnp.dot(pieces[0], pieces[1].T, preferred_element_type=jnp.float32)
        return total + term.astype(jnp.bfloat16).astype(jnp.float32), None

    start = jnp.zeros((NQ, NTRAIN), jnp.float32)
    total, unused = lax.scan(add_group, start, (query_groups, train_groups))
    return total
```

```python
import itertools

import jax
import jax.numpy as jnp
from jax import lax
from jax.sharding import Mesh, PartitionSpec as P

NAMES = ("h", "z", "c", "l", "x")
SIZES = (2, 8, 2, 2, 4)


def move(value, target):
    pairs = []
    for place in itertools.product(*map(range, SIZES)):
        to = target(*place)
        if to is not None:
            pairs.append((flat(place), flat(to)))
    return lax.ppermute(value, NAMES, pairs)


def flat(place):
    index = 0
    for at, size in zip(place, SIZES, strict=True):
        index = index * size + at % size
    return index


def other_core(value):
    return move(value, lambda h, z, c, l, x: (h, z, 1 - c, l, x))


def other_half(value):
    return move(value, lambda h, z, c, l, x: (1 - h, z, c, l, x))


def other_run(value):
    return move(value, lambda h, z, c, l, x: (h, z, c, 1 - l, x))


def along_z(value):
    return move(value, lambda h, z, c, l, x: (h, z + (1 if c == 0 else -1), c, l, x))


def first_x(value):
    return move(value, lambda h, z, c, l, x: (h, z, c, l, x ^ (1 if c == 0 else 3)))


def second_x(value):
    return move(value, lambda h, z, c, l, x: (h, z, c, l, x ^ (3 if c == 0 else 1)))


def prepare(rows, blocks):
    size = blocks.shape[1]
    parts = [
        jnp.dot(
            rows[:, b * size : (b + 1) * size], blocks[b], preferred_element_type=jnp.float32
        ).astype(jnp.bfloat16)
        for b in range(blocks.shape[0])
    ]
    return jnp.concatenate(parts, axis=1)


def score_rows(ready, train_grads):
    return lax.dot_general(
        ready, train_grads, (((1,), (1,)), ((), ())), preferred_element_type=jnp.float32
    )


def both_cores(c, mine, theirs):
    return jnp.where(
        c == 0, jnp.concatenate([mine, theirs]), jnp.concatenate([theirs, mine])
    )


def gather_planes(c, plane):
    rows = plane.shape[0]
    one = along_z(plane)
    two = along_z(one)
    three = along_z(two)
    half = lax.dynamic_slice_in_dim(three, c * (rows // 2), rows // 2)
    four = along_z(half)
    odd = jnp.concatenate([one, three])
    odd_theirs = other_core(odd)
    even = jnp.concatenate([two, four])
    even_theirs = other_core(even)
    far = both_cores(c, even[rows:], even_theirs[rows:])
    odd_set = jnp.concatenate([odd, odd_theirs])
    even_set = jnp.concatenate([plane, even[:rows], even_theirs[:rows], far])
    return odd_set, even_set


def reduce_x(x, c, block, train_grads):
    m1 = jnp.where(c == 0, 1, 3)
    m2 = jnp.where(c == 0, 3, 1)
    sent = jnp.concatenate([block(x ^ m1), block(x ^ 2)])
    kept = jnp.concatenate([block(x), block(x ^ m2)])
    rows = kept.shape[0] // 2
    come = first_x(score_rows(sent, train_grads).astype(jnp.bfloat16))
    kept = lax.optimization_barrier(score_rows(kept, train_grads))
    total = kept + come.astype(jnp.float32)
    come = second_x(total[rows:].astype(jnp.bfloat16))
    return total[:rows] + come.astype(jnp.float32)


def on_device(train_grads, query_grads, precond):
    h, z, c, l, x = (lax.axis_index(name) for name in NAMES)
    mine = prepare(query_grads, precond)
    rows = 2 * mine.shape[0]
    across = other_half(mine)
    plane = both_cores(c, mine, other_core(mine))
    plane_across = both_cores(c, across, other_core(across))

    def odd_place(owner):
        step = (2 * owner + 1 - z % 2 - z) % 8
        near = (step == 1) | (step == 7)
        above = step < 4
        own = above == (c == 1)
        return jnp.where(own, 0, 2) + jnp.where(near, 0, 1)

    def even_place(owner):
        step = (2 * owner + z % 2 - z) % 8
        own = (step == 2) == (c == 1)
        return jnp.where(step == 0, 0, jnp.where(step == 4, 3, jnp.where(own, 1, 2)))

    sums = []
    for start in (plane, plane_across):
        odd_set, even_set = gather_planes(c, start)
        for held, place in ((odd_set, odd_place), (even_set, even_place)):
            block = lambda owner: lax.dynamic_slice_in_dim(held, place(owner) * rows, rows)
            sums.append(reduce_x(x, c, block, train_grads))
    odd, even, odd_across, even_across = sums

    def over_runs(own, across):
        sent = jnp.where(l == h, across, own).astype(jnp.bfloat16)
        kept = jnp.where(l == h, own, across)
        return kept + other_run(sent).astype(jnp.float32)

    odd = over_runs(odd, odd_across)
    even = over_runs(even, even_across)
    return jnp.where(z % 2 == 0, jnp.concatenate([even, odd]), jnp.concatenate([odd, even]))


def solution(mesh):
    wide = Mesh(mesh.devices.reshape(SIZES), NAMES)
    ex, lb = NAMES[:3], NAMES[3:]
    placed = (P(ex, lb), P(ex, lb), P(lb, None, None))
    return jax.shard_map(
        on_device, mesh=wide, in_specs=placed, out_specs=P(lb, ex), check_vma=False
    )
```

```python
import itertools

import jax
import jax.numpy as jnp
from jax import lax
from jax.sharding import Mesh, PartitionSpec as P

NAMES = ("h", "z", "c", "l", "x")
SIZES = (2, 8, 2, 2, 4)


def move(value, target):
    pairs = []
    for place in itertools.product(*map(range, SIZES)):
        to = target(*place)
        if to is not None:
            pairs.append((flat(place), flat(to)))
    return lax.ppermute(value, NAMES, pairs)


def flat(place):
    index = 0
    for at, size in zip(place, SIZES, strict=True):
        index = index * size + at % size
    return index


def other_core(value):
    return move(value, lambda h, z, c, l, x: (h, z, 1 - c, l, x))


def other_half(value):
    return move(value, lambda h, z, c, l, x: (1 - h, z, c, l, x))


def other_run(value):
    return move(value, lambda h, z, c, l, x: (h, z, c, 1 - l, x))


def along_z_twice(value):
    return move(value, lambda h, z, c, l, x: (h, z + (2 if c == 0 else -2), c, l, x))


def along_z(value):
    return move(value, lambda h, z, c, l, x: (h, z + (1 if c == 0 else -1), c, l, x))


def first_x(value):
    return move(value, lambda h, z, c, l, x: (h, z, c, l, x ^ (1 if c == 0 else 3)))


def second_x(value):
    return move(value, lambda h, z, c, l, x: (h, z, c, l, x ^ (3 if c == 0 else 1)))


def prepare(rows, blocks):
    count = rows.shape[0]
    split = rows.reshape(count, blocks.shape[0], blocks.shape[1])
    mixed = jnp.einsum("rbi,bij->rbj", split, blocks, preferred_element_type=jnp.float32)
    return mixed.reshape(count, -1).astype(jnp.bfloat16)


def score_rows(ready, train_grads):
    return lax.dot_general(
        ready, train_grads, (((1,), (1,)), ((), ())), preferred_element_type=jnp.float32
    ).astype(jnp.bfloat16)


def both_cores(c, mine, theirs):
    return jnp.where(
        c == 0, jnp.concatenate([mine, theirs]), jnp.concatenate([theirs, mine])
    )


def together(*values):
    return lax.optimization_barrier(values)


def on_device(train_grads, query_grads, precond):
    h, z, c, l, x = (lax.axis_index(name) for name in NAMES)
    m1 = jnp.where(c == 0, 1, 3)
    m2 = jnp.where(c == 0, 3, 1)

    mine = prepare(query_grads, precond)
    theirs = other_core(mine)
    plane = both_cores(c, mine, theirs)
    rows = plane.shape[0]
    part = rows // 2
    own_rows = lambda held: lax.dynamic_slice_in_dim(held, c * part, part)

    def scores(place, cuts, *blocks):
        held = jnp.concatenate(blocks)
        size = rows // cuts
        picked = [
            lax.dynamic_slice_in_dim(held, place(owner) * rows + cut * size, size)
            for cut in range(cuts)
            for owner in (x ^ m1, x ^ 2, x, x ^ m2)
        ]
        return score_rows(jnp.concatenate(picked), train_grads)

    def odd_place(owner):
        step = (2 * owner + 1 - z % 2 - z) % 8
        near = (step == 1) | (step == 7)
        above = step < 4
        own = above == (c == 1)
        return jnp.where(own, 0, 1) + jnp.where(near, 0, 2)

    def even_place(owner):
        step = (2 * owner + z % 2 - z) % 8
        own = (step == 2) == (c == 1)
        return jnp.where(step == 0, 0, jnp.where(step == 4, 3, jnp.where(own, 1, 2)))

    mine, plane = together(mine, plane)
    across, o1 = together(other_half(mine), along_z(plane))
    o2 = along_z(o1)
    a0 = both_cores(c, across, other_core(across))
    a1 = along_z(a0)
    a2 = along_z_twice(a0)
    o3 = along_z(o2)
    a3 = along_z(a2)
    a4 = along_z_twice(own_rows(a2))
    o4 = along_z(own_rows(o3))
    t1, t2, t3 = map(other_core, (o1, o2, o3))
    odd = scores(odd_place, 1, o1, t1, o3, t3)
    odd_come, odd = first_x(odd[: 2 * rows]), odd[2 * rows :]
    a3, a4, o4, odd = together(a3, a4, o4, odd)
    t4 = other_core(o4)
    even = scores(even_place, 2, plane, o2, t2, both_cores(c, o4, t4))
    u1, u2, u3, u4 = map(other_core, (a1, a2, a3, a4))
    odd_across = scores(odd_place, 1, a1, u1, a3, u3)
    even_across = scores(even_place, 2, a0, a2, u2, both_cores(c, a4, u4))

    wide = lambda value: value.astype(jnp.float32)

    def pass_on(total, sizes):
        parts, at = [], 0
        for size in sizes:
            parts.append((total[at : at + size], total[at + size : at + 2 * size]))
            at += 2 * size
        come = second_x(jnp.concatenate([sent for _, sent in parts]).astype(jnp.bfloat16))
        sums, at = [], 0
        for (kept, _), size in zip(parts, sizes, strict=True):
            sums.append(kept + wide(come[at : at + size]))
            at += size
        return sums

    def over_runs(own, across):
        sent = jnp.where(l == h, across, own).astype(jnp.bfloat16)
        kept = jnp.where(l == h, own, across)
        return wide(kept) + wide(other_run(sent))

    half = 2 * rows
    (odd,) = pass_on(wide(odd) + wide(odd_come), [rows])
    second = over_runs(even[half:], even_across[half:])
    second_come = first_x(second[:rows].astype(jnp.bfloat16))
    come = first_x(odd_across[:half])
    (odd_across,) = pass_on(wide(odd_across[half:]) + wide(come), [rows])
    come = first_x(jnp.concatenate([even[:rows], even_across[:rows]]))
    kept = jnp.concatenate([even[rows:half], even_across[rows:half]])
    even, even_across = pass_on(wide(kept) + wide(come), [part, part])
    (second,) = pass_on(second[rows:] + wide(second_come), [part])

    odd = over_runs(odd, odd_across)
    even = jnp.concatenate([over_runs(even, even_across), second])
    return jnp.where(z % 2 == 0, jnp.concatenate([even, odd]), jnp.concatenate([odd, even]))


def solution(mesh):
    wide = Mesh(mesh.devices.reshape(SIZES), NAMES)
    ex, lb = NAMES[:3], NAMES[3:]
    placed = (P(ex, lb), P(ex, lb), P(lb, None, None))
    return jax.shard_map(
        on_device, mesh=wide, in_specs=placed, out_specs=P(lb, ex), check_vma=False
    )
```

```python
import itertools

import jax
import jax.numpy as jnp
from jax import lax
from jax.sharding import Mesh, PartitionSpec as P

NAMES = ("h", "z", "c", "l", "x")
SIZES = (2, 8, 2, 2, 4)


def move(value, target):
    pairs = []
    for place in itertools.product(*map(range, SIZES)):
        to = target(*place)
        if to is not None:
            pairs.append((flat(place), flat(to)))
    return lax.ppermute(value, NAMES, pairs)


def flat(place):
    index = 0
    for at, size in zip(place, SIZES, strict=True):
        index = index * size + at % size
    return index


def other_core(value):
    return move(value, lambda h, z, c, l, x: (h, z, 1 - c, l, x))


def other_half(value):
    return move(value, lambda h, z, c, l, x: (1 - h, z, c, l, x))


def other_run(value):
    return move(value, lambda h, z, c, l, x: (h, z, c, 1 - l, x))


def along_z_twice(value):
    return move(value, lambda h, z, c, l, x: (h, z + (2 if c == 0 else -2), c, l, x))


def along_z(value):
    return move(value, lambda h, z, c, l, x: (h, z + (1 if c == 0 else -1), c, l, x))


def first_x(value):
    return move(value, lambda h, z, c, l, x: (h, z, c, l, x ^ (1 if c == 0 else 3)))


def second_x(value):
    return move(value, lambda h, z, c, l, x: (h, z, c, l, x ^ (3 if c == 0 else 1)))


def prepare(rows, blocks):
    count = rows.shape[0]
    split = rows.reshape(count, blocks.shape[0], blocks.shape[1])
    mixed = jnp.einsum("rbi,bij->rbj", split, blocks, preferred_element_type=jnp.float32)
    return mixed.reshape(count, -1).astype(jnp.bfloat16)


def score_rows(ready, train_grads):
    return lax.dot_general(
        ready, train_grads, (((1,), (1,)), ((), ())), preferred_element_type=jnp.float32
    ).astype(jnp.bfloat16)


def both_cores(c, mine, theirs):
    return jnp.where(
        c == 0, jnp.concatenate([mine, theirs]), jnp.concatenate([theirs, mine])
    )


def together(*values):
    return lax.optimization_barrier(values)


def on_device(train_grads, query_grads, precond):
    h, z, c, l, x = (lax.axis_index(name) for name in NAMES)
    m1 = jnp.where(c == 0, 1, 3)
    m2 = jnp.where(c == 0, 3, 1)

    mine = prepare(query_grads, precond)
    theirs = other_core(mine)
    plane = both_cores(c, mine, theirs)
    rows = plane.shape[0]
    part = rows // 2
    own_rows = lambda held: lax.dynamic_slice_in_dim(held, c * part, part)

    def picked(place, cuts, *blocks):
        held = jnp.concatenate(blocks)
        size = rows // cuts
        return jnp.concatenate(
            [
                lax.dynamic_slice_in_dim(held, place(owner) * rows + cut * size, size)
                for cut in range(cuts)
                for owner in (x ^ m1, x ^ 2, x, x ^ m2)
            ]
        )

    def scores(ready):
        return score_rows(ready, train_grads)

    def odd_place(owner):
        step = (2 * owner + 1 - z % 2 - z) % 8
        near = (step == 1) | (step == 7)
        above = step < 4
        own = above == (c == 1)
        return jnp.where(own, 0, 1) + jnp.where(near, 0, 2)

    def even_place(owner):
        step = (2 * owner + z % 2 - z) % 8
        own = (step == 2) == (c == 1)
        return jnp.where(step == 0, 0, jnp.where(step == 4, 3, jnp.where(own, 1, 2)))

    mine, plane = together(mine, plane)
    across, o1 = together(other_half(mine), along_z(plane))
    o2 = along_z(o1)
    a0 = both_cores(c, across, other_core(across))
    t1, t2 = other_core(o1), other_core(o2)
    known = scores(jnp.concatenate([plane, o2, t2]))
    known = [known[:rows], known[rows : 2 * rows], known[2 * rows :]]
    a1 = along_z(a0)
    a2, known[1] = together(along_z_twice(a0), known[1])
    o3 = along_z(o2)
    a3 = along_z(a2)
    a4 = along_z_twice(own_rows(a2))
    o4 = along_z(own_rows(o3))
    t3 = other_core(o3)
    odd = scores(picked(odd_place, 1, o1, t1, o3, t3))
    odd_come, odd = first_x(odd[: 2 * rows]), odd[2 * rows :]
    a3, a4, o4, odd = together(a3, a4, o4, odd)
    t4 = other_core(o4)
    u1, u2, u3, u4 = map(other_core, (a1, a2, a3, a4))
    odd_across = scores(picked(odd_place, 1, a1, u1, a3, u3))
    u4, odd_across_kept = together(u4, odd_across[2 * rows :])
    ready = picked(even_place, 2, a0, a2, u2, both_cores(c, a4, u4))
    even_across = scores(jnp.concatenate([ready, both_cores(c, o4, t4)]))
    even = picked(even_place, 2, *known, even_across[4 * rows :])

    wide = lambda value: value.astype(jnp.float32)

    def pass_on(total, sizes):
        parts, at = [], 0
        for size in sizes:
            parts.append((total[at : at + size], total[at + size : at + 2 * size]))
            at += 2 * size
        come = second_x(jnp.concatenate([sent for _, sent in parts]).astype(jnp.bfloat16))
        sums, at = [], 0
        for (kept, _), size in zip(parts, sizes, strict=True):
            sums.append(kept + wide(come[at : at + size]))
            at += size
        return sums

    def over_runs(own, across):
        sent = jnp.where(l == h, across, own).astype(jnp.bfloat16)
        kept = jnp.where(l == h, own, across)
        return wide(kept) + wide(other_run(sent))

    half = 2 * rows
    (odd,) = pass_on(wide(odd) + wide(odd_come), [rows])
    second = over_runs(even[half:], even_across[half : 2 * half])
    second_come = first_x(second[:rows].astype(jnp.bfloat16))
    come = first_x(odd_across[:half])
    (odd_across,) = pass_on(wide(odd_across_kept) + wide(come), [rows])
    come = first_x(jnp.concatenate([even[:rows], even_across[:rows]]))
    kept = jnp.concatenate([even[rows:half], even_across[rows:half]])
    even, even_across = pass_on(wide(kept) + wide(come), [part, part])
    (second,) = pass_on(second[rows:] + wide(second_come), [part])

    odd = over_runs(odd, odd_across)
    even = jnp.concatenate([over_runs(even, even_across), second])
    return jnp.where(z % 2 == 0, jnp.concatenate([even, odd]), jnp.concatenate([odd, even]))


def solution(mesh):
    wide = Mesh(mesh.devices.reshape(SIZES), NAMES)
    ex, lb = NAMES[:3], NAMES[3:]
    placed = (P(ex, lb), P(ex, lb), P(lb, None, None))
    return jax.shard_map(
        on_device, mesh=wide, in_specs=placed, out_specs=P(lb, ex), check_vma=False
    )
```

```python
import itertools

import jax
import jax.numpy as jnp
from jax import lax
from jax.sharding import Mesh, PartitionSpec as P

NAMES = ("h", "z", "c", "l", "x")
SIZES = (2, 8, 2, 2, 4)


def move(value, target):
    pairs = []
    for place in itertools.product(*map(range, SIZES)):
        to = target(*place)
        if to is not None:
            pairs.append((flat(place), flat(to)))
    return lax.ppermute(value, NAMES, pairs)


def flat(place):
    index = 0
    for at, size in zip(place, SIZES, strict=True):
        index = index * size + at % size
    return index


def other_core(value):
    return move(value, lambda h, z, c, l, x: (h, z, 1 - c, l, x))


def other_half(value):
    return move(value, lambda h, z, c, l, x: (1 - h, z, c, l, x))


def other_run(value):
    return move(value, lambda h, z, c, l, x: (h, z, c, 1 - l, x))


def along_z_twice(value):
    return move(value, lambda h, z, c, l, x: (h, z + (2 if c == 0 else -2), c, l, x))


def along_z(value):
    return move(value, lambda h, z, c, l, x: (h, z + (1 if c == 0 else -1), c, l, x))


def first_x(value):
    return move(value, lambda h, z, c, l, x: (h, z, c, l, x ^ (1 if c == 0 else 3)))


def second_x(value):
    return move(value, lambda h, z, c, l, x: (h, z, c, l, x ^ (3 if c == 0 else 1)))


def prepare(rows, blocks):
    count = rows.shape[0]
    split = rows.reshape(count, blocks.shape[0], blocks.shape[1])
    mixed = jnp.einsum("rbi,bij->rbj", split, blocks, preferred_element_type=jnp.float32)
    return mixed.reshape(count, -1).astype(jnp.bfloat16)


def score_rows(ready, train_grads):
    return lax.dot_general(
        ready, train_grads, (((1,), (1,)), ((), ())), preferred_element_type=jnp.float32
    ).astype(jnp.bfloat16)


def both_cores(c, mine, theirs):
    return jnp.where(
        c == 0, jnp.concatenate([mine, theirs]), jnp.concatenate([theirs, mine])
    )


def together(*values):
    return lax.optimization_barrier(values)


def on_device(train_grads, query_grads, precond):
    h, z, c, l, x = (lax.axis_index(name) for name in NAMES)
    m1 = jnp.where(c == 0, 1, 3)
    m2 = jnp.where(c == 0, 3, 1)

    mine = prepare(query_grads, precond)
    theirs = other_core(mine)
    plane = both_cores(c, mine, theirs)
    rows = plane.shape[0]
    part = rows // 2
    own_rows = lambda held: lax.dynamic_slice_in_dim(held, c * part, part)

    def picked(place, cuts, *blocks):
        held = jnp.concatenate(blocks)
        size = rows // cuts
        return jnp.concatenate(
            [
                lax.dynamic_slice_in_dim(held, place(owner) * rows + cut * size, size)
                for cut in range(cuts)
                for owner in (x ^ m1, x ^ 2, x, x ^ m2)
            ]
        )

    def scores(ready):
        return score_rows(ready, train_grads)

    def odd_place(owner):
        step = (2 * owner + 1 - z % 2 - z) % 8
        near = (step == 1) | (step == 7)
        above = step < 4
        own = above == (c == 1)
        return jnp.where(own, 0, 1) + jnp.where(near, 0, 2)

    def even_place(owner):
        step = (2 * owner + z % 2 - z) % 8
        own = (step == 2) == (c == 1)
        return jnp.where(step == 0, 0, jnp.where(step == 4, 3, jnp.where(own, 1, 2)))

    mine, plane = together(mine, plane)
    across = other_half(mine)
    theirs = other_core(across)
    across, o1 = together(across, along_z(plane))
    o2 = along_z(o1)
    a0 = both_cores(c, across, theirs)
    t1, t2 = other_core(o1), other_core(o2)
    known = scores(jnp.concatenate([plane, o2, t2]))
    known = [known[:rows], known[rows : 2 * rows], known[2 * rows :]]
    a1, known[0] = together(along_z(a0), known[0])
    a2, known[1] = together(along_z_twice(a0), known[1])
    o3 = along_z(o2)
    a3 = along_z(a2)
    a4 = along_z_twice(own_rows(a2))
    o4 = along_z_twice(own_rows(o2))
    t3 = other_core(o3)
    odd = scores(picked(odd_place, 1, o1, t1, o3, t3))
    odd_come, odd = first_x(odd[: 2 * rows]), odd[2 * rows :]
    a3, a4, o4, odd = together(a3, a4, o4, odd)
    t4 = other_core(o4)
    u1, u2, u3, u4 = map(other_core, (a1, a2, a3, a4))
    odd_across = scores(picked(odd_place, 1, a1, u1, a3, u3))
    u4, odd_across_kept = together(u4, odd_across[2 * rows :])
    ready = picked(even_place, 2, a0, a2, u2, both_cores(c, a4, u4))
    even_across = scores(jnp.concatenate([ready, both_cores(c, o4, t4)]))
    even = picked(even_place, 2, *known, even_across[4 * rows :])

    wide = lambda value: value.astype(jnp.float32)

    def pass_on(total, sizes):
        parts, at = [], 0
        for size in sizes:
            parts.append((total[at : at + size], total[at + size : at + 2 * size]))
            at += 2 * size
        come = second_x(jnp.concatenate([sent for _, sent in parts]).astype(jnp.bfloat16))
        sums, at = [], 0
        for (kept, _), size in zip(parts, sizes, strict=True):
            sums.append(kept + wide(come[at : at + size]))
            at += size
        return sums

    def over_runs(own, across):
        sent = jnp.where(l == h, across, own).astype(jnp.bfloat16)
        kept = jnp.where(l == h, own, across)
        return wide(kept) + wide(other_run(sent))

    half = 2 * rows
    (odd,) = pass_on(wide(odd) + wide(odd_come), [rows])
    second = over_runs(even[half:], even_across[half : 2 * half])
    second_come = first_x(second[:rows].astype(jnp.bfloat16))
    come = first_x(odd_across[:half])
    (odd_across,) = pass_on(wide(odd_across_kept) + wide(come), [rows])
    come = first_x(jnp.concatenate([even[:rows], even_across[:rows]]))
    kept = jnp.concatenate([even[rows:half], even_across[rows:half]])
    even, even_across = pass_on(wide(kept) + wide(come), [part, part])
    (second,) = pass_on(second[rows:] + wide(second_come), [part])

    odd = over_runs(odd, odd_across)
    even = jnp.concatenate([over_runs(even, even_across), second])
    return jnp.where(z % 2 == 0, jnp.concatenate([even, odd]), jnp.concatenate([odd, even]))


def solution(mesh):
    wide = Mesh(mesh.devices.reshape(SIZES), NAMES)
    ex, lb = NAMES[:3], NAMES[3:]
    placed = (P(ex, lb), P(ex, lb), P(lb, None, None))
    return jax.shard_map(
        on_device, mesh=wide, in_specs=placed, out_specs=P(lb, ex), check_vma=False
    )
```

```python
import itertools

import jax
import jax.numpy as jnp
from jax import lax
from jax.sharding import Mesh, PartitionSpec as P

NAMES = ("h", "z", "c", "l", "x")
SIZES = (2, 8, 2, 2, 4)


def move(value, target):
    pairs = []
    for place in itertools.product(*map(range, SIZES)):
        to = target(*place)
        if to is not None:
            pairs.append((flat(place), flat(to)))
    return lax.ppermute(value, NAMES, pairs)


def flat(place):
    index = 0
    for at, size in zip(place, SIZES, strict=True):
        index = index * size + at % size
    return index


def other_core(value):
    return move(value, lambda h, z, c, l, x: (h, z, 1 - c, l, x))


def other_half(value):
    return move(value, lambda h, z, c, l, x: (1 - h, z, c, l, x))


def other_run(value):
    return move(value, lambda h, z, c, l, x: (h, z, c, 1 - l, x))


def along_z_twice(value):
    return move(value, lambda h, z, c, l, x: (h, z + (2 if c == 0 else -2), c, l, x))


def along_z(value):
    return move(value, lambda h, z, c, l, x: (h, z + (1 if c == 0 else -1), c, l, x))


def first_x(value):
    return move(value, lambda h, z, c, l, x: (h, z, c, l, x ^ (1 if c == 0 else 3)))


def second_x(value):
    return move(value, lambda h, z, c, l, x: (h, z, c, l, x ^ (3 if c == 0 else 1)))


def prepare(rows, blocks):
    count = rows.shape[0]
    split = rows.reshape(count, blocks.shape[0], blocks.shape[1])
    mixed = jnp.einsum("rbi,bij->rbj", split, blocks, preferred_element_type=jnp.float32)
    return mixed.reshape(count, -1).astype(jnp.bfloat16)


def score_rows(ready, train_grads):
    return lax.dot_general(
        ready, train_grads, (((1,), (1,)), ((), ())), preferred_element_type=jnp.float32
    ).astype(jnp.bfloat16)


def both_cores(c, mine, theirs):
    return jnp.where(
        c == 0, jnp.concatenate([mine, theirs]), jnp.concatenate([theirs, mine])
    )


def together(*values):
    return lax.optimization_barrier(values)


def on_device(train_grads, query_grads, precond):
    h, z, c, l, x = (lax.axis_index(name) for name in NAMES)
    m1 = jnp.where(c == 0, 1, 3)
    m2 = jnp.where(c == 0, 3, 1)

    mine = prepare(query_grads, precond)
    theirs = other_core(mine)
    plane = both_cores(c, mine, theirs)
    rows = plane.shape[0]
    part = rows // 2
    own_rows = lambda held: lax.dynamic_slice_in_dim(held, c * part, part)

    def picked(place, cuts, *blocks):
        held = jnp.concatenate(blocks)
        size = rows // cuts
        return jnp.concatenate(
            [
                lax.dynamic_slice_in_dim(held, place(owner) * rows + cut * size, size)
                for cut in range(cuts)
                for owner in (x ^ m1, x ^ 2, x, x ^ m2)
            ]
        )

    def scores(ready):
        return score_rows(ready, train_grads)

    def odd_place(owner):
        step = (2 * owner + 1 - z % 2 - z) % 8
        near = (step == 1) | (step == 7)
        above = step < 4
        own = above == (c == 1)
        return jnp.where(own, 0, 1) + jnp.where(near, 0, 2)

    def even_place(owner):
        step = (2 * owner + z % 2 - z) % 8
        own = (step == 2) == (c == 1)
        return jnp.where(step == 0, 0, jnp.where(step == 4, 3, jnp.where(own, 1, 2)))

    mine, plane = together(mine, plane)
    across = other_half(mine)
    theirs = other_core(across)
    across, o1 = together(across, along_z(plane))
    o2 = along_z(o1)
    a0 = both_cores(c, across, theirs)
    t1, t2 = other_core(o1), other_core(o2)
    known = scores(jnp.concatenate([plane, o2, t2]))
    known = [known[:rows], known[rows : 2 * rows], known[2 * rows :]]
    a1, known[0] = together(along_z(a0), known[0])
    a2, known[1] = together(along_z_twice(a0), known[1])
    o3 = along_z(o2)
    a3 = along_z(a2)
    a4 = along_z_twice(own_rows(a2))
    o4 = along_z_twice(own_rows(o2))
    t3 = other_core(o3)
    odd = scores(picked(odd_place, 1, o1, t1, o3, t3))
    odd_come, odd = first_x(odd[: 2 * rows]), odd[2 * rows :]
    a3, a4, o4, odd = together(a3, a4, o4, odd)
    u1, u2, u3 = map(other_core, (a1, a2, a3))
    swapped = other_core(jnp.concatenate([a4, o4]))
    u4, t4 = swapped[:part], swapped[part:]
    odd_across = scores(picked(odd_place, 1, a1, u1, a3, u3))
    u4, odd_across_kept = together(u4, odd_across[2 * rows :])
    ready = picked(even_place, 2, a0, a2, u2, both_cores(c, a4, u4))
    even_across = scores(jnp.concatenate([ready, both_cores(c, o4, t4)]))
    even = picked(even_place, 2, *known, even_across[4 * rows :])

    wide = lambda value: value.astype(jnp.float32)

    def pass_on(total, sizes):
        parts, at = [], 0
        for size in sizes:
            parts.append((total[at : at + size], total[at + size : at + 2 * size]))
            at += 2 * size
        come = second_x(jnp.concatenate([sent for _, sent in parts]).astype(jnp.bfloat16))
        sums, at = [], 0
        for (kept, _), size in zip(parts, sizes, strict=True):
            sums.append(kept + wide(come[at : at + size]))
            at += size
        return sums

    def over_runs(own, across):
        sent = jnp.where(l == h, across, own).astype(jnp.bfloat16)
        kept = jnp.where(l == h, own, across)
        return wide(kept) + wide(other_run(sent))

    half = 2 * rows
    (odd,) = pass_on(wide(odd) + wide(odd_come), [rows])
    second = over_runs(even[half:], even_across[half : 2 * half])
    second_come = first_x(second[:rows].astype(jnp.bfloat16))
    come = first_x(odd_across[:half])
    (odd_across,) = pass_on(wide(odd_across_kept) + wide(come), [rows])
    come = first_x(jnp.concatenate([even[:rows], even_across[:rows]]))
    kept = jnp.concatenate([even[rows:half], even_across[rows:half]])
    even, even_across = pass_on(wide(kept) + wide(come), [part, part])
    (second,) = pass_on(second[rows:] + wide(second_come), [part])

    odd = over_runs(odd, odd_across)
    even = jnp.concatenate([over_runs(even, even_across), second])
    return jnp.where(z % 2 == 0, jnp.concatenate([even, odd]), jnp.concatenate([odd, even]))


def solution(mesh):
    wide = Mesh(mesh.devices.reshape(SIZES), NAMES)
    ex, lb = NAMES[:3], NAMES[3:]
    placed = (P(ex, lb), P(ex, lb), P(lb, None, None))
    return jax.shard_map(
        on_device, mesh=wide, in_specs=placed, out_specs=P(lb, ex), check_vma=False
    )
```
